32 devices in a mesh: req: 4 (over y, x), grp: 8 (over z, core).
Axes of the slice: x: 2, y: 2, z: 4, core: 2. Of those that a mesh axis runs over, the one named last changes fastest.
Arguments:
- residual: bfloat16 [4, 8, 128, 4096], P('req', 'grp'), may hold values from -64 to 64
- suffix_proj: bfloat16 [4, 8, 3, 128, 4096], P('req', 'grp'), may hold values from -256 to 256
- prefix_cache: bfloat16 [4, 8, 2, 128, 4096], P('req', 'grp'), may hold values from -8 to 8
- owner_req: int32 [8], replicated, may hold values from 0 to 3, as said below
- lengths: int32 [4, 8], P('req', 'grp'), may hold values from 8 to 128, as said below
- norm_gain: float32 [4096], replicated, may hold values from 0.1 to 1.9
- up_weight: bfloat16 [12288, 4096], P('grp'), may hold values from -0.09375 to 0.09375
- down_weight: bfloat16 [12288, 4096], P('grp'), may hold values from -0.0546875 to 0.0546875
Outputs:
- output: bfloat16 [4, 8, 128, 4096], P('req', 'grp')
The draws below stay inside these ranges and needn't reach their ends.
Inputs may be any that keep to these rules, and one draw needn't show every extreme that they name: owner_req[g] is the req index whose cache block holds group g's prefix. The first lengths[r, g] of the 128 slots of a request are live; in every req index one request fills all 128 slots.
All inputs are finite; a program needn't handle non-finite values.
Results may differ from the reference program's by a relative error of at most 0.014.
Values may be sent and summed in bfloat16 or wider, within the bound.
A program may use at most 128 MiB of HBM per device.

```python
import math
import jax
import jax.numpy as jnp
from jax import lax

D = 4096
HEADS = 32
HEAD_DIM = 128
UNITS = 12288
SLOTS = 128
PREFIX = 128
N_REQ = 4
N_GRP = 8


def owner_table(key):
    return jax.random.randint(jax.random.fold_in(key, 101), (N_GRP,), 0, N_REQ).astype(jnp.int32)


def prefix_table(key):
    sampled = jnp.clip(jax.random.normal(jax.random.fold_in(key, 202), (N_REQ, N_GRP, 2, PREFIX, D), jnp.float32), -6.0, 6.0)
    return sampled


def suffix_table(key):
    sampled = jnp.clip(jax.random.normal(jax.random.fold_in(key, 303), (N_REQ, N_GRP, 3, SLOTS, D), jnp.float32), -6.0, 6.0)
    return sampled


def draw_owner_req(key, part):
    return owner_table(key)


def draw_prefix_cache(key, part):
    return prefix_table(key).astype(jnp.bfloat16)


def draw_suffix_proj(key, part):
    return suffix_table(key).astype(jnp.bfloat16)


def draw_lengths(key, part):
    sampled = jax.random.randint(jax.random.fold_in(key, 404), (N_REQ, N_GRP), 8, SLOTS + 1)
    full_column = jax.random.randint(jax.random.fold_in(key, 405), (N_REQ,), 0, N_GRP)
    columns = jnp.arange(N_GRP, dtype=jnp.int32)[None, :]
    return jnp.where(columns == full_column[:, None], SLOTS, sampled).astype(jnp.int32)


def draw_residual(key, part):
    sampled = jnp.clip(jax.random.normal(jax.random.fold_in(key, 505), (N_REQ, N_GRP, SLOTS, D), jnp.float32), -6.0, 6.0)
    return sampled.astype(jnp.bfloat16)


def levels(key, dims, split, smallest, high):
    gain, own = 1.0, jax.random.fold_in(key, 6)
    for axis_at, parts in split:
        draws = jnp.exp(jax.random.uniform(jax.random.fold_in(own, axis_at), (parts,), jnp.float32, smallest / len(split), high / len(split)))
        gain = gain * jnp.repeat(draws, dims[axis_at] // parts).reshape([-1 if axis == axis_at else 1 for axis in range(len(dims))])
    return gain


def noise(own_key, dims, scale, reach, pieces=(), kind=jnp.bfloat16):
    values = scale * jax.random.normal(own_key, dims, jnp.float32)
    if pieces:
        values = values * levels(own_key, dims, pieces, -0.22, 0.18)
    return jnp.clip(values, -reach, reach).astype(kind)


def setup_inputs(seed: int = 0) -> dict:
    keys = jax.random.split(jax.random.key(seed), 9)
    residual = draw_residual(jax.random.fold_in(keys[8], 71), 0)
    suffix_proj = draw_suffix_proj(jax.random.fold_in(keys[8], 71), 0)
    prefix_cache = draw_prefix_cache(jax.random.fold_in(keys[8], 71), 0)
    owner_req = draw_owner_req(jax.random.fold_in(keys[8], 71), 0)
    lengths = draw_lengths(jax.random.fold_in(keys[8], 71), 0)
    norm_gain = jnp.clip(1.0 + 0.18 * jax.random.normal(keys[5], (D,), jnp.float32), 0.1, 1.9)
    up_weight = noise(keys[6], (UNITS, D), D ** -0.5, 0.09375, ((0, 8),))
    down_weight = noise(keys[7], (UNITS, D), UNITS ** -0.5, 0.0546875, ((0, 8),))
    return {"residual": residual, "suffix_proj": suffix_proj, "prefix_cache": prefix_cache, "owner_req": owner_req, "lengths": lengths, "norm_gain": norm_gain, "up_weight": up_weight, "down_weight": down_weight}


NORM_EPS = 1e-05

def head_slopes():
    return jnp.exp2(-8.0 * jnp.arange(1, HEADS + 1, dtype=jnp.float32) / HEADS)

def attend(queries, key_rows, value_rows, key_pos, query_pos, causal):
    scores = jnp.einsum('qhe,khe->hqk', queries.astype(jnp.float32), key_rows.astype(jnp.float32))
    scores = scores * (1.0 / math.sqrt(HEAD_DIM))
    offsets = (key_pos[None, :] - query_pos[:, None]).astype(jnp.float32)
    scores = scores + head_slopes()[:, None, None] * offsets[None, :, :]
    if causal:
        scores = jnp.where((key_pos[None, :] <= query_pos[:, None])[None], scores, -jnp.inf)
    row_max = lax.optimization_barrier(jnp.max(scores, axis=2))
    weights = jnp.exp(scores - row_max[:, :, None])
    row_total = lax.optimization_barrier(jnp.sum(weights, axis=2))
    rounded = lax.optimization_barrier(weights.astype(jnp.bfloat16)).astype(jnp.float32)
    context = jnp.einsum('hqk,khe->qhe', rounded, value_rows.astype(jnp.float32))
    return (row_max, row_total, context)

def merge_parts(first, second):
    joint_max = jnp.maximum(first[0], second[0])
    first_scale = jnp.exp(first[0] - joint_max)
    second_scale = jnp.exp(second[0] - joint_max)
    numer = first[2] * first_scale.T[:, :, None] + second[2] * second_scale.T[:, :, None]
    denom = first[1] * first_scale + second[1] * second_scale
    merged = numer / denom.T[:, :, None]
    return merged.reshape(merged.shape[0], merged.shape[1] * merged.shape[2])

def layer_norm(state, norm_gain):
    values = state.astype(jnp.float32)
    center = values - lax.optimization_barrier(jnp.mean(values, axis=-1, keepdims=True))
    spread = lax.optimization_barrier(jnp.mean(center * center, axis=-1, keepdims=True))
    return (center * lax.rsqrt(spread + NORM_EPS) * norm_gain).astype(jnp.bfloat16)

def reference(residual, suffix_proj, prefix_cache, owner_req, lengths, norm_gain, up_weight, down_weight):
    query_pos = PREFIX + jnp.arange(SLOTS, dtype=jnp.int32)
    prefix_pos = jnp.arange(PREFIX, dtype=jnp.int32)

    def one_device(device_index):
        req_index = device_index // N_GRP
        group_index = device_index % N_GRP
        block = suffix_proj[req_index, group_index].reshape(3, SLOTS, HEADS, HEAD_DIM)
        cached = prefix_cache[owner_req[group_index], group_index].reshape(2, PREFIX, HEADS, HEAD_DIM)
        first = attend(block[0], cached[0], cached[1], prefix_pos, query_pos, False)
        second = attend(block[0], block[1], block[2], query_pos, query_pos, True)
        context = merge_parts(first, second)
        return (residual[req_index, group_index].astype(jnp.float32) + context).astype(jnp.bfloat16)
    states = lax.map(one_device, jnp.arange(N_REQ * N_GRP, dtype=jnp.int32))
    token_states = states.reshape(N_REQ * N_GRP * SLOTS, D)
    normed = layer_norm(token_states, norm_gain)
    share = UNITS // N_GRP

    def add_class(class_index, running):
        offset = (class_index * share).astype(jnp.int32)
        up_rows = lax.dynamic_slice_in_dim(up_weight, offset, share, 0)
        down_rows = lax.dynamic_slice_in_dim(down_weight, offset, share, 0)
        preactivation = lax.dot_general(normed, up_rows, (((1,), (1,)), ((), ())), preferred_element_type=jnp.float32)
        hidden = jax.nn.gelu(preactivation, approximate=False).astype(jnp.bfloat16)
        partial_term = jnp.dot(hidden, down_rows, preferred_element_type=jnp.float32).astype(jnp.bfloat16)
        return running + partial_term.astype(jnp.float32)
    mlp_sum = lax.fori_loop(0, N_GRP, add_class, jnp.zeros((N_REQ * N_GRP * SLOTS, D), jnp.float32))
    live = jnp.arange(SLOTS, dtype=jnp.int32)[None, None, :] < lengths[:, :, None]
    combined = states.reshape(N_REQ, N_GRP, SLOTS, D).astype(jnp.float32) + mlp_sum.reshape(N_REQ, N_GRP, SLOTS, D)
    return jnp.where(live[..., None], combined, 0.0).astype(jnp.bfloat16)
```

```python
import functools
import math

import jax
import jax.numpy as jnp
from jax import lax
from jax.experimental import pallas as pl
from jax.experimental.pallas import tpu as pltpu
from jax.sharding import PartitionSpec as P

HEADS = 32


NORM_EPS = 1e-05


def swap_halves(half, bits, req_size, owner_index):
    mine = lax.axis_index("req")
    for bit in bits:
        pairs = [(r, r ^ (1 << bit)) for r in range(req_size)]
        other = lax.ppermute(half, "req", pairs)
        same = ((mine >> bit) & 1) == ((owner_index >> bit) & 1)
        half = jnp.where(same, half, other)
    return half


def from_owner(block, req_size, owner_index):
    bits = list(range(req_size.bit_length() - 1))
    keys = swap_halves(block[0], bits, req_size, owner_index)
    values = swap_halves(block[1], bits[::-1], req_size, owner_index)
    return keys, values


def head_slopes(head_count):
    return jnp.exp2(-8.0 * jnp.arange(1, head_count + 1, dtype=jnp.float32) / head_count)


def attend(queries, key_rows, value_rows, key_pos, query_pos, causal):
    head_size = queries.shape[2]
    scores = jnp.einsum("qhe,khe->hqk", queries, key_rows, preferred_element_type=jnp.float32)
    scores = scores * (1.0 / math.sqrt(head_size))
    offsets = (key_pos[None, :] - query_pos[:, None]).astype(jnp.float32)
    scores = scores + head_slopes(queries.shape[1])[:, None, None] * offsets[None, :, :]
    if causal:
        scores = jnp.where((key_pos[None, :] <= query_pos[:, None])[None], scores, -jnp.inf)
    row_max = jnp.max(scores, axis=2)
    weights = jnp.exp(scores - row_max[:, :, None])
    row_total = jnp.sum(weights, axis=2)
    context = jnp.einsum(
        "hqk,khe->qhe", weights.astype(jnp.bfloat16), value_rows, preferred_element_type=jnp.float32
    )
    return (row_max, row_total, context)


def merge_parts(first, second):
    joint_max = jnp.maximum(first[0], second[0])
    first_scale = jnp.exp(first[0] - joint_max)
    second_scale = jnp.exp(second[0] - joint_max)
    numer = first[2] * first_scale.T[:, :, None] + second[2] * second_scale.T[:, :, None]
    denom = first[1] * first_scale + second[1] * second_scale
    merged = numer / denom.T[:, :, None]
    return merged.reshape(merged.shape[0], merged.shape[1] * merged.shape[2])


def layer_norm(state, norm_gain):
    values = state.astype(jnp.float32)
    center = values - jnp.mean(values, axis=-1, keepdims=True)
    spread = jnp.mean(center * center, axis=-1, keepdims=True)
    return (center * lax.rsqrt(spread + NORM_EPS) * norm_gain).astype(jnp.bfloat16)


MESH = pl.DeviceIdType.MESH
AG_PARTS = 2
RS_PARTS = 4
UP_TILE = 512
DOWN_TILE = 512


def mlp_kernel(
    chips, normed_hbm, state_ref, up_hbm, down_hbm, out_ref,
    xg, upv, dnv, hid, part, sib, line,
    wsem, ag_recv, ag_send, sib_send, sib_recv, rs_send, rs_recv,
):
    rows = xg.shape[2]
    width = xg.shape[3]
    units = upv.shape[0]
    ag_rows = rows // AG_PARTS
    rs_rows = rows // RS_PARTS
    me = lax.axis_index("grp")
    z = me // 2
    c = me % 2
    twin = z * 2 + 1 - c
    has_left = z > 0
    has_right = z < chips - 1

    up_copy = pltpu.make_async_copy(up_hbm, upv, wsem.at[0])
    down_copy = pltpu.make_async_copy(down_hbm, dnv, wsem.at[1])
    own_copy = pltpu.make_async_copy(normed_hbm, xg.at[z, c], wsem.at[2])
    own_copy.start()
    up_copy.start()
    down_copy.start()

    barrier = pltpu.get_barrier_semaphore()
    pl.semaphore_signal(barrier, inc=1, device_id={"grp": twin}, device_id_type=MESH)

    @pl.when(has_left)
    def _():
        pl.semaphore_signal(barrier, inc=1, device_id={"grp": me - 2}, device_id_type=MESH)

    @pl.when(has_right)
    def _():
        pl.semaphore_signal(barrier, inc=1, device_id={"grp": me + 2}, device_id_type=MESH)

    @pl.when(jnp.logical_and(has_left, has_right))
    def _():
        pl.semaphore_wait(barrier, 3)

    @pl.when(jnp.logical_not(jnp.logical_and(has_left, has_right)))
    def _():
        pl.semaphore_wait(barrier, 2)

    own_copy.wait()

    def ag_copy(zb, cc, s, way, target):
        piece = xg.at[zb, cc, pl.ds(s * ag_rows, ag_rows)]
        return pltpu.make_async_remote_copy(
            src_ref=piece, dst_ref=piece,
            send_sem=ag_send.at[way, zb, s], recv_sem=ag_recv.at[zb, cc, s],
            device_id={"grp": target}, device_id_type=MESH,
        )

    def sib_copy(zb):
        return pltpu.make_async_remote_copy(
            src_ref=part.at[zb, 1 - c], dst_ref=sib.at[zb],
            send_sem=sib_send.at[zb], recv_sem=sib_recv.at[zb],
            device_id={"grp": twin}, device_id_type=MESH,
        )

    def rs_copy(zb, slot, q, target):
        span = pl.ds(q * rs_rows, rs_rows)
        return pltpu.make_async_remote_copy(
            src_ref=part.at[zb, c, span], dst_ref=line.at[slot, span],
            send_sem=rs_send.at[zb, q], recv_sem=rs_recv.at[slot, q],
            device_id={"grp": target}, device_id_type=MESH,
        )

    for s in range(AG_PARTS):
        @pl.when(has_right)
        def _():
            ag_copy(z, c, s, 0, me + 2).start()

        @pl.when(has_left)
        def _():
            ag_copy(z, c, s, 1, me - 2).start()

        ag_copy(z, c, s, 2, twin).start()

    up_copy.wait()
    down_copy.wait()

    def compute(zb):
        for s in range(AG_PARTS):
            ag_copy(zb, 1 - c, s, 2, twin).wait_recv()

        def up_step(j, carry):
            cols = pl.ds(pl.multiple_of(j * UP_TILE, UP_TILE), UP_TILE)
            pre = lax.dot_general(
                xg[zb].reshape(2 * rows, width), upv[cols, :],
                (((1,), (1,)), ((), ())), preferred_element_type=jnp.float32,
            )
            act = 0.5 * pre * (1.0 + lax.erf(pre * math.sqrt(0.5)))
            hid[:, cols] = act.astype(jnp.bfloat16)
            return carry

        lax.fori_loop(0, units // UP_TILE, up_step, 0)

        def down_step(j, carry):
            cols = pl.ds(pl.multiple_of(j * DOWN_TILE, DOWN_TILE), DOWN_TILE)
            term = jnp.dot(hid[...], dnv[:, cols], preferred_element_type=jnp.float32)
            part[zb, :, :, cols] = term.astype(jnp.bfloat16).reshape(2, rows, DOWN_TILE)
            return carry

        lax.fori_loop(0, width // DOWN_TILE, down_step, 0)
        sib_copy(zb).start()

    def add_line(zb, q, with_line):
        span = pl.ds(q * rs_rows, rs_rows)
        total = part[zb, c, span].astype(jnp.float32) + sib[zb, span].astype(jnp.float32)
        if with_line:
            total = total + line[zb, span].astype(jnp.float32)
        part[zb, c, span] = total.astype(jnp.bfloat16)

    def step(d, carry):
        low, high = z - d, z + d
        for s in range(AG_PARTS):
            @pl.when(jnp.logical_and(d > 0, low >= 0))
            def _():
                ag_copy(low, c, s, 0, twin).wait_recv()

                @pl.when(has_right)
                def _():
                    ag_copy(low, c, s, 0, me + 2).start()

                ag_copy(low, c, s, 2, twin).start()

            @pl.when(jnp.logical_and(d > 0, high < chips))
            def _():
                ag_copy(high, c, s, 1, twin).wait_recv()

                @pl.when(has_left)
                def _():
                    ag_copy(high, c, s, 1, me - 2).start()

                ag_copy(high, c, s, 2, twin).start()

        def side_step(side, inner):
            zb = z - d + 2 * d * side

            @pl.when(jnp.logical_and(jnp.logical_and(zb >= 0, zb < chips), d + 1 > side))
            def _():
                compute(zb)

            return inner

        lax.fori_loop(0, 2, side_step, 0)

        to_right = d
        to_left = chips - 1 - d
        goes_right = z < to_right
        goes_left = z > to_left

        @pl.when(goes_right)
        def _():
            sib_copy(to_right).wait_recv()

        @pl.when(goes_left)
        def _():
            sib_copy(to_left).wait_recv()

        for q in range(RS_PARTS):
            @pl.when(goes_right)
            def _():
                @pl.when(has_left)
                def _():
                    rs_copy(to_right, to_right, q, twin).wait_recv()
                    add_line(to_right, q, True)

                @pl.when(jnp.logical_not(has_left))
                def _():
                    add_line(to_right, q, False)

                rs_copy(to_right, to_right, q, me + 2).start()

            @pl.when(goes_left)
            def _():
                @pl.when(has_right)
                def _():
                    rs_copy(to_left, to_left, q, twin).wait_recv()
                    add_line(to_left, q, True)

                @pl.when(jnp.logical_not(has_right))
                def _():
                    add_line(to_left, q, False)

                @pl.when(z - 1 == to_left)
                def _():
                    rs_copy(to_left, chips, q, me - 2).start()

                @pl.when(z - 1 > to_left)
                def _():
                    rs_copy(to_left, to_left, q, me - 2).start()

        return carry

    lax.fori_loop(0, chips, step, 0)

    sib_copy(z).wait_recv()
    for q in range(RS_PARTS):
        span = pl.ds(q * rs_rows, rs_rows)

        @pl.when(has_left)
        def _():
            rs_copy(z, z, q, twin).wait_recv()

        @pl.when(has_right)
        def _():
            rs_copy(z, chips, q, twin).wait_recv()

        def finish(slots):
            total = part[z, c, span].astype(jnp.float32) + sib[z, span].astype(jnp.float32)
            for slot in slots:
                total = total + line[slot, span].astype(jnp.float32)
            total = total + state_ref[span].astype(jnp.float32)
            out_ref[span] = total.astype(jnp.bfloat16)

        @pl.when(jnp.logical_and(has_left, has_right))
        def _():
            finish([z, chips])

        @pl.when(jnp.logical_not(has_left))
        def _():
            finish([chips])

        @pl.when(jnp.logical_not(has_right))
        def _():
            finish([z])

    def drain(zb, carry):
        for s in range(AG_PARTS):
            @pl.when(jnp.logical_and(has_right, zb <= z))
            def _():
                ag_copy(zb, c, s, 0, twin).wait_send()

            @pl.when(jnp.logical_and(has_left, zb >= z))
            def _():
                ag_copy(zb, c, s, 1, twin).wait_send()

            ag_copy(zb, c, s, 2, twin).wait_send()
        sib_copy(zb).wait_send()
        for q in range(RS_PARTS):
            @pl.when(zb != z)
            def _():
                rs_copy(zb, zb, q, twin).wait_send()
        return carry

    lax.fori_loop(0, chips, drain, 0)


def mlp_bytes(grp_size, rows, width, units):
    chips = grp_size // 2
    blocks = 2 * chips + 2 * chips + chips + chips + 1 + 4
    return 2 * width * (blocks * rows + 2 * units) + 4 * rows * units


VMEM_LIMIT = 60 * 1024 * 1024


def mlp_fused(grp_size, normed, states, up_weight, down_weight):
    chips = grp_size // 2
    rows, width = normed.shape
    units = up_weight.shape[0]
    bf16 = jnp.bfloat16
    dma = pltpu.SemaphoreType.DMA
    total_rows = rows * grp_size
    return pl.pallas_call(
        functools.partial(mlp_kernel, chips),
        out_shape=jax.ShapeDtypeStruct((rows, width), bf16),
        in_specs=[
            pl.BlockSpec(memory_space=pl.ANY),
            pl.BlockSpec(memory_space=pltpu.VMEM),
            pl.BlockSpec(memory_space=pl.ANY),
            pl.BlockSpec(memory_space=pl.ANY),
        ],
        out_specs=pl.BlockSpec(memory_space=pltpu.VMEM),
        scratch_shapes=[
            pltpu.VMEM((chips, 2, rows, width), bf16),
            pltpu.VMEM((units, width), bf16),
            pltpu.VMEM((units, width), bf16),
            pltpu.VMEM((2 * rows, units), bf16),
            pltpu.VMEM((chips, 2, rows, width), bf16),
            pltpu.VMEM((chips, rows, width), bf16),
            pltpu.VMEM((chips + 1, rows, width), bf16),
            dma((3,)),
            dma((chips, 2, AG_PARTS)),
            dma((3, chips, AG_PARTS)),
            dma((chips,)),
            dma((chips,)),
            dma((chips, RS_PARTS)),
            dma((chips + 1, RS_PARTS)),
        ],
        compiler_params=pltpu.CompilerParams(
            collective_id=0, has_side_effects=True, vmem_limit_bytes=VMEM_LIMIT
        ),
        cost_estimate=pl.CostEstimate(
            flops=4 * total_rows * width * units,
            bytes_accessed=4 * units * width,
            transcendentals=total_rows * units,
        ),
    )(normed, states, up_weight, down_weight)


def mlp_plain(normed, states, up_weight, down_weight):
    preactivation = lax.dot_general(
        lax.all_gather(normed, "grp", axis=0, tiled=True),
        up_weight,
        (((1,), (1,)), ((), ())),
        preferred_element_type=jnp.float32,
    )
    hidden = jax.nn.gelu(preactivation, approximate=False).astype(jnp.bfloat16)
    partial_term = jnp.dot(hidden, down_weight, preferred_element_type=jnp.float32).astype(
        jnp.bfloat16
    )
    mlp_sum = lax.psum_scatter(partial_term, "grp", scatter_dimension=0, tiled=True)
    return (states.astype(jnp.float32) + mlp_sum.astype(jnp.float32)).astype(jnp.bfloat16)


def body(
    req_size, grp_size,
    residual, suffix_proj, prefix_cache, owner_req, lengths, norm_gain, up_weight, down_weight
):
    slot_count = residual.shape[2]
    feature_count = residual.shape[3]
    prefix_count = prefix_cache.shape[3]
    head_count = HEADS
    head_size = feature_count // head_count
    block = suffix_proj[0, 0].reshape(3, slot_count, head_count, head_size)
    query_pos = prefix_count + jnp.arange(slot_count, dtype=jnp.int32)
    prefix_pos = jnp.arange(prefix_count, dtype=jnp.int32)
    group_index = lax.axis_index("grp")
    owner_index = lax.dynamic_index_in_dim(owner_req, group_index, 0, keepdims=False)
    cached = from_owner(prefix_cache[0, 0], req_size, owner_index)
    cached = [half.reshape(prefix_count, head_count, head_size) for half in cached]
    first = attend(block[0], cached[0], cached[1], prefix_pos, query_pos, False)
    second = attend(block[0], block[1], block[2], query_pos, query_pos, True)
    context = merge_parts(first, second)
    states = (residual[0, 0].astype(jnp.float32) + context).astype(jnp.bfloat16)
    normed = layer_norm(states, norm_gain)
    if mlp_bytes(grp_size, slot_count, feature_count, up_weight.shape[0]) <= VMEM_LIMIT * 15 // 16:
        combined = mlp_fused(grp_size, normed, states, up_weight, down_weight)
    else:
        combined = mlp_plain(normed, states, up_weight, down_weight)
    live = jnp.arange(slot_count, dtype=jnp.int32) < lengths[0, 0]
    output = jnp.where(live[:, None], combined, jnp.zeros_like(combined))
    return output[None, None]


def solution(mesh):
    placed = (
        P("req", "grp", None, None),
        P("req", "grp", None, None, None),
        P("req", "grp", None, None, None),
        P(),
        P("req", "grp"),
        P(),
        P("grp", None),
        P("grp", None),
    )
    return jax.shard_map(
        functools.partial(body, mesh.shape["req"], mesh.shape["grp"]),
        mesh=mesh, in_specs=placed, out_specs=P("req", "grp", None, None), check_vma=False
    )
```

```python
import functools
import math

import jax
import jax.numpy as jnp
from jax import lax
from jax.experimental import pallas as pl
from jax.experimental.pallas import tpu as pltpu
from jax.sharding import PartitionSpec as P

HEADS = 32


NORM_EPS = 1e-05


def swap_halves(half, bits, req_size, owner_index):
    mine = lax.axis_index("req")
    for bit in bits:
        pairs = [(r, r ^ (1 << bit)) for r in range(req_size)]
        other = lax.ppermute(half, "req", pairs)
        same = ((mine >> bit) & 1) == ((owner_index >> bit) & 1)
        half = jnp.where(same, half, other)
    return half


def from_owner(block, req_size, owner_index):
    bits = list(range(req_size.bit_length() - 1))
    keys = swap_halves(block[0], bits, req_size, owner_index)
    values = swap_halves(block[1], bits[::-1], req_size, owner_index)
    return keys, values


def head_slopes(head_count):
    return jnp.exp2(-8.0 * jnp.arange(1, head_count + 1, dtype=jnp.float32) / head_count)


def attend(queries, key_rows, value_rows, key_pos, query_pos, causal):
    head_size = queries.shape[2]
    scores = jnp.einsum("qhe,khe->hqk", queries, key_rows, preferred_element_type=jnp.float32)
    scores = scores * (1.0 / math.sqrt(head_size))
    offsets = (key_pos[None, :] - query_pos[:, None]).astype(jnp.float32)
    scores = scores + head_slopes(queries.shape[1])[:, None, None] * offsets[None, :, :]
    if causal:
        scores = jnp.where((key_pos[None, :] <= query_pos[:, None])[None], scores, -jnp.inf)
    row_max = jnp.max(scores, axis=2)
    weights = jnp.exp(scores - row_max[:, :, None])
    row_total = jnp.sum(weights, axis=2)
    context = jnp.einsum(
        "hqk,khe->qhe", weights.astype(jnp.bfloat16), value_rows, preferred_element_type=jnp.float32
    )
    return (row_max, row_total, context)


def merge_parts(first, second):
    joint_max = jnp.maximum(first[0], second[0])
    first_scale = jnp.exp(first[0] - joint_max)
    second_scale = jnp.exp(second[0] - joint_max)
    numer = first[2] * first_scale.T[:, :, None] + second[2] * second_scale.T[:, :, None]
    denom = first[1] * first_scale + second[1] * second_scale
    merged = numer / denom.T[:, :, None]
    return merged.reshape(merged.shape[0], merged.shape[1] * merged.shape[2])


def layer_norm(state, norm_gain):
    values = state.astype(jnp.float32)
    center = values - jnp.mean(values, axis=-1, keepdims=True)
    spread = jnp.mean(center * center, axis=-1, keepdims=True)
    return (center * lax.rsqrt(spread + NORM_EPS) * norm_gain).astype(jnp.bfloat16)


MESH = pl.DeviceIdType.MESH
AG_PARTS = 4
RS_PARTS = 4
UP_TILE = 512
DOWN_TILE = 512


def layer_kernel(
    chips, owner_ref, slope_ref, gain_ref, residual_ref, proj_hbm, cache_hbm, up_hbm, down_hbm,
    out_ref,
    xg, upv, dnv, hid, part, sib, line, xn, values_two,
    wsem, ag_recv, ag_send, sib_send, sib_recv, rs_send, rs_recv, swap_send, swap_recv,
):
    rows = xg.shape[2]
    width = xg.shape[3]
    units = upv.shape[0]
    ag_cols = width // AG_PARTS
    rs_rows = rows // RS_PARTS
    me = lax.axis_index("grp")
    z = me // 2
    c = me % 2
    twin = z * 2 + 1 - c
    has_left = z > 0
    has_right = z < chips - 1

    up_copy = pltpu.make_async_copy(up_hbm, upv, wsem.at[0])
    down_copy = pltpu.make_async_copy(down_hbm, dnv, wsem.at[1])
    queries, keys, values = part.at[0, 0], part.at[0, 1], part.at[1, 0]
    keys_own, values_own = part.at[1, 1], part.at[2, 0]
    keys_one, values_one, keys_two = part.at[2, 1], part.at[3, 0], part.at[3, 1]
    loads = [
        pltpu.make_async_copy(cache_hbm.at[0], keys_own, wsem.at[2]),
        pltpu.make_async_copy(cache_hbm.at[1], values_own, wsem.at[3]),
        pltpu.make_async_copy(proj_hbm.at[0], queries, wsem.at[4]),
        pltpu.make_async_copy(proj_hbm.at[1], keys, wsem.at[5]),
        pltpu.make_async_copy(proj_hbm.at[2], values, wsem.at[6]),
    ]
    for load in loads:
        load.start()

    r = lax.axis_index("req")
    low_bit, high_bit = r % 2, r // 2
    peer_low = r + 1 - 2 * low_bit
    peer_high = r + 2 - 4 * high_bit
    owner = owner_ref[me]
    same_low = (owner % 2) == low_bit
    same_high = (owner // 2) == high_bit

    barrier = pltpu.get_barrier_semaphore()
    pl.semaphore_signal(barrier, inc=1, device_id={"grp": twin}, device_id_type=MESH)
    for peer in (peer_low, peer_high):
        pl.semaphore_signal(barrier, inc=1, device_id={"req": peer}, device_id_type=MESH)

    @pl.when(has_left)
    def _():
        pl.semaphore_signal(barrier, inc=1, device_id={"grp": me - 2}, device_id_type=MESH)

    @pl.when(has_right)
    def _():
        pl.semaphore_signal(barrier, inc=1, device_id={"grp": me + 2}, device_id_type=MESH)

    @pl.when(jnp.logical_and(has_left, has_right))
    def _():
        pl.semaphore_wait(barrier, 5)

    @pl.when(jnp.logical_not(jnp.logical_and(has_left, has_right)))
    def _():
        pl.semaphore_wait(barrier, 4)

    def swap_copy(kind, i):
        cols = pl.ds(i * ag_cols, ag_cols)
        src, dst, peer = (
            (keys_own, keys_one, peer_low),
            (values_own, values_one, peer_high),
            (keys_one, keys_two, peer_high),
            (values_one, values_two, peer_low),
        )[kind]
        return pltpu.make_async_remote_copy(
            src_ref=src.at[:, cols], dst_ref=dst.at[:, cols],
            send_sem=swap_send.at[kind, i], recv_sem=swap_recv.at[kind, i],
            device_id={"req": peer}, device_id_type=MESH,
        )

    def swap_start(i):
        swap_copy(0, i).start()
        swap_copy(1, i).start()

    def swap_relay(i):
        cols = pl.ds(i * ag_cols, ag_cols)
        swap_copy(0, i).wait_recv()
        keys_one[:, cols] = lax.select(same_low, keys_own[:, cols], keys_one[:, cols])
        swap_copy(2, i).start()
        swap_copy(1, i).wait_recv()
        values_one[:, cols] = lax.select(same_high, values_own[:, cols], values_one[:, cols])
        swap_copy(3, i).start()
        if i + 2 < AG_PARTS:
            swap_start(i + 2)

    loads[0].wait()
    loads[1].wait()
    swap_start(0)
    swap_start(1)
    for load in loads[2:]:
        load.wait()
    up_copy.start()
    down_copy.start()

    def ag_copy(zb, cc, s, way, target):
        piece = xg.at[zb, cc, :, pl.ds(s * ag_cols, ag_cols)]
        return pltpu.make_async_remote_copy(
            src_ref=piece, dst_ref=piece,
            send_sem=ag_send.at[way, zb, s], recv_sem=ag_recv.at[zb, cc, s],
            device_id={"grp": target}, device_id_type=MESH,
        )

    def sib_copy(zb):
        return pltpu.make_async_remote_copy(
            src_ref=part.at[zb, 1 - c], dst_ref=sib.at[zb],
            send_sem=sib_send.at[zb], recv_sem=sib_recv.at[zb],
            device_id={"grp": twin}, device_id_type=MESH,
        )

    def rs_copy(zb, slot, q, target):
        span = pl.ds(q * rs_rows, rs_rows)
        return pltpu.make_async_remote_copy(
            src_ref=part.at[zb, c, span], dst_ref=line.at[slot, span],
            send_sem=rs_send.at[zb, q], recv_sem=rs_recv.at[slot, q],
            device_id={"grp": target}, device_id_type=MESH,
        )

    query_at = lax.broadcasted_iota(jnp.int32, (rows, rows), 0)
    key_at = lax.broadcasted_iota(jnp.int32, (rows, rows), 1)
    offset = (key_at - query_at).astype(jnp.float32)
    causal = key_at <= query_at
    head_size = width // HEADS
    scale = 1.0 / math.sqrt(head_size)
    nt = (((1,), (1,)), ((), ()))

    def attend_head(h, carry):
        cols = pl.ds(pl.multiple_of(h * head_size, head_size), head_size)
        slope = slope_ref[h]
        query = queries[:, cols]
        old_keys = lax.select(same_high, keys_one[:, cols], keys_two[:, cols])
        old_values = lax.select(same_low, values_one[:, cols], values_two[:, cols])
        old = lax.dot_general(query, old_keys, nt, preferred_element_type=jnp.float32)
        new = lax.dot_general(query, keys[:, cols], nt, preferred_element_type=jnp.float32)
        old = old * scale + slope * (offset - float(rows))
        new = jnp.where(causal, new * scale + slope * offset, -jnp.inf)
        top = jnp.maximum(
            jnp.max(old, axis=1, keepdims=True), jnp.max(new, axis=1, keepdims=True)
        )
        old = jnp.exp(old - top)
        new = jnp.exp(new - top)
        total = jnp.sum(old, axis=1, keepdims=True) + jnp.sum(new, axis=1, keepdims=True)
        context = jnp.dot(
            old.astype(jnp.bfloat16), old_values, preferred_element_type=jnp.float32
        ) + jnp.dot(
            new.astype(jnp.bfloat16), values[:, cols], preferred_element_type=jnp.float32
        )
        state = residual_ref[:, cols].astype(jnp.float32) + context / total
        xg[z, c, :, cols] = state.astype(jnp.bfloat16)
        return carry

    heads = HEADS // AG_PARTS
    swap_relay(0)
    for s in range(AG_PARTS):
        if s + 1 < AG_PARTS:
            swap_relay(s + 1)
        swap_copy(2, s).wait_recv()
        swap_copy(3, s).wait_recv()
        lax.fori_loop(s * heads, (s + 1) * heads, attend_head, 0, unroll=2)

        @pl.when(has_right)
        def _():
            ag_copy(z, c, s, 0, me + 2).start()

        @pl.when(has_left)
        def _():
            ag_copy(z, c, s, 1, me - 2).start()

        ag_copy(z, c, s, 2, twin).start()

    for s in range(AG_PARTS):
        for kind in range(4):
            swap_copy(kind, s).wait_send()
    up_copy.wait()
    down_copy.wait()

    def compute(zb):
        for s in range(AG_PARTS):
            ag_copy(zb, 1 - c, s, 2, twin).wait_recv()

        def norm_step(t, carry):
            span = pl.ds(pl.multiple_of((t % (rows // 16)) * 16, 16), 16)
            dest = pl.ds(pl.multiple_of(t * 16, 16), 16)
            raw = xg[zb, t // (rows // 16), span, :].astype(jnp.float32)
            center = raw - jnp.mean(raw, axis=1, keepdims=True)
            spread = jnp.mean(center * center, axis=1, keepdims=True)
            scaled = center * lax.rsqrt(spread + NORM_EPS) * gain_ref[...]
            xn[dest, :] = scaled.astype(jnp.bfloat16)
            return carry

        lax.fori_loop(0, 2 * rows // 16, norm_step, 0)

        def up_step(j, carry):
            cols = pl.ds(pl.multiple_of(j * UP_TILE, UP_TILE), UP_TILE)
            pre = lax.dot_general(
                xn[...], upv[cols, :],
                (((1,), (1,)), ((), ())), preferred_element_type=jnp.float32,
            )
            act = 0.5 * pre * (1.0 + lax.erf(pre * math.sqrt(0.5)))
            hid[:, cols] = act.astype(jnp.bfloat16)
            return carry

        lax.fori_loop(0, units // UP_TILE, up_step, 0)

        def down_step(j, carry):
            cols = pl.ds(pl.multiple_of(j * DOWN_TILE, DOWN_TILE), DOWN_TILE)
            term = jnp.dot(hid[...], dnv[:, cols], preferred_element_type=jnp.float32)
            part[zb, :, :, cols] = term.astype(jnp.bfloat16).reshape(2, rows, DOWN_TILE)
            return carry

        lax.fori_loop(0, width // DOWN_TILE, down_step, 0)
        sib_copy(zb).start()

    def add_line(zb, q, with_line):
        span = pl.ds(q * rs_rows, rs_rows)
        total = part[zb, c, span].astype(jnp.float32) + sib[zb, span].astype(jnp.float32)
        if with_line:
            total = total + line[zb, span].astype(jnp.float32)
        part[zb, c, span] = total.astype(jnp.bfloat16)

    def step(d, carry):
        low, high = z - d, z + d
        for s in range(AG_PARTS):
            @pl.when(jnp.logical_and(d > 0, low >= 0))
            def _():
                ag_copy(low, c, s, 0, twin).wait_recv()

                @pl.when(has_right)
                def _():
                    ag_copy(low, c, s, 0, me + 2).start()

                ag_copy(low, c, s, 2, twin).start()

            @pl.when(jnp.logical_and(d > 0, high < chips))
            def _():
                ag_copy(high, c, s, 1, twin).wait_recv()

                @pl.when(has_left)
                def _():
                    ag_copy(high, c, s, 1, me - 2).start()

                ag_copy(high, c, s, 2, twin).start()

        def side_step(side, inner):
            zb = z - d + 2 * d * side

            @pl.when(jnp.logical_and(jnp.logical_and(zb >= 0, zb < chips), d + 1 > side))
            def _():
                compute(zb)

            return inner

        lax.fori_loop(0, 2, side_step, 0)

        to_right = d
        to_left = chips - 1 - d
        goes_right = z < to_right
        goes_left = z > to_left

        @pl.when(goes_right)
        def _():
            sib_copy(to_right).wait_recv()

        @pl.when(goes_left)
        def _():
            sib_copy(to_left).wait_recv()

        for q in range(RS_PARTS):
            @pl.when(goes_right)
            def _():
                @pl.when(has_left)
                def _():
                    rs_copy(to_right, to_right, q, twin).wait_recv()
                    add_line(to_right, q, True)

                @pl.when(jnp.logical_not(has_left))
                def _():
                    add_line(to_right, q, False)

                rs_copy(to_right, to_right, q, me + 2).start()

            @pl.when(goes_left)
            def _():
                @pl.when(has_right)
                def _():
                    rs_copy(to_left, to_left, q, twin).wait_recv()
                    add_line(to_left, q, True)

                @pl.when(jnp.logical_not(has_right))
                def _():
                    add_line(to_left, q, False)

                @pl.when(z - 1 == to_left)
                def _():
                    rs_copy(to_left, chips, q, me - 2).start()

                @pl.when(z - 1 > to_left)
                def _():
                    rs_copy(to_left, to_left, q, me - 2).start()

        return carry

    lax.fori_loop(0, chips, step, 0)

    sib_copy(z).wait_recv()
    for q in range(RS_PARTS):
        span = pl.ds(q * rs_rows, rs_rows)

        @pl.when(has_left)
        def _():
            rs_copy(z, z, q, twin).wait_recv()

        @pl.when(has_right)
        def _():
            rs_copy(z, chips, q, twin).wait_recv()

        def finish(slots):
            total = part[z, c, span].astype(jnp.float32) + sib[z, span].astype(jnp.float32)
            for slot in slots:
                total = total + line[slot, span].astype(jnp.float32)
            total = total + xg[z, c, span, :].astype(jnp.float32)
            out_ref[span] = total.astype(jnp.bfloat16)

        @pl.when(jnp.logical_and(has_left, has_right))
        def _():
            finish([z, chips])

        @pl.when(jnp.logical_not(has_left))
        def _():
            finish([chips])

        @pl.when(jnp.logical_not(has_right))
        def _():
            finish([z])

    def drain(zb, carry):
        for s in range(AG_PARTS):
            @pl.when(jnp.logical_and(has_right, zb <= z))
            def _():
                ag_copy(zb, c, s, 0, twin).wait_send()

            @pl.when(jnp.logical_and(has_left, zb >= z))
            def _():
                ag_copy(zb, c, s, 1, twin).wait_send()

            ag_copy(zb, c, s, 2, twin).wait_send()
        sib_copy(zb).wait_send()
        for q in range(RS_PARTS):
            @pl.when(zb != z)
            def _():
                rs_copy(zb, zb, q, twin).wait_send()
        return carry

    lax.fori_loop(0, chips, drain, 0)


def layer_bytes(grp_size, rows, width, units):
    chips = grp_size // 2
    blocks = 2 * chips + 2 * chips + chips + chips + 1 + 5
    return 2 * width * (blocks * rows + 2 * units) + 4 * rows * units


VMEM_LIMIT = 60 * 1024 * 1024


def layer_fused(
    grp_size, owner_req, norm_gain, residual, suffix_proj, prefix_cache, up_weight, down_weight
):
    chips = grp_size // 2
    rows, width = residual.shape
    units = up_weight.shape[0]
    bf16 = jnp.bfloat16
    dma = pltpu.SemaphoreType.DMA
    total_rows = rows * grp_size
    return pl.pallas_call(
        functools.partial(layer_kernel, chips),
        out_shape=jax.ShapeDtypeStruct((rows, width), bf16),
        in_specs=[
            pl.BlockSpec(memory_space=pltpu.SMEM),
            pl.BlockSpec(memory_space=pltpu.SMEM),
            pl.BlockSpec(memory_space=pltpu.VMEM),
            pl.BlockSpec(memory_space=pltpu.VMEM),
            pl.BlockSpec(memory_space=pl.ANY),
            pl.BlockSpec(memory_space=pl.ANY),
            pl.BlockSpec(memory_space=pl.ANY),
            pl.BlockSpec(memory_space=pl.ANY),
        ],
        out_specs=pl.BlockSpec(memory_space=pltpu.VMEM),
        scratch_shapes=[
            pltpu.VMEM((chips, 2, rows, width), bf16),
            pltpu.VMEM((units, width), bf16),
            pltpu.VMEM((units, width), bf16),
            pltpu.VMEM((2 * rows, units), bf16),
            pltpu.VMEM((chips, 2, rows, width), bf16),
            pltpu.VMEM((chips, rows, width), bf16),
            pltpu.VMEM((chips + 1, rows, width), bf16),
            pltpu.VMEM((2 * rows, width), bf16),
            pltpu.VMEM((rows, width), bf16),
            dma((7,)),
            dma((chips, 2, AG_PARTS)),
            dma((3, chips, AG_PARTS)),
            dma((chips,)),
            dma((chips,)),
            dma((chips, RS_PARTS)),
            dma((chips + 1, RS_PARTS)),
            dma((4, AG_PARTS)),
            dma((4, AG_PARTS)),
        ],
        compiler_params=pltpu.CompilerParams(
            collective_id=0, has_side_effects=True, vmem_limit_bytes=VMEM_LIMIT
        ),
        cost_estimate=pl.CostEstimate(
            flops=4 * total_rows * width * units,
            bytes_accessed=4 * units * width,
            transcendentals=total_rows * units,
        ),
    )(
        owner_req, head_slopes(HEADS), norm_gain[None, :], residual, suffix_proj, prefix_cache,
        up_weight, down_weight,
    )


def mlp_plain(normed, states, up_weight, down_weight):
    preactivation = lax.dot_general(
        lax.all_gather(normed, "grp", axis=0, tiled=True),
        up_weight,
        (((1,), (1,)), ((), ())),
        preferred_element_type=jnp.float32,
    )
    hidden = jax.nn.gelu(preactivation, approximate=False).astype(jnp.bfloat16)
    partial_term = jnp.dot(hidden, down_weight, preferred_element_type=jnp.float32).astype(
        jnp.bfloat16
    )
    mlp_sum = lax.psum_scatter(partial_term, "grp", scatter_dimension=0, tiled=True)
    return (states.astype(jnp.float32) + mlp_sum.astype(jnp.float32)).astype(jnp.bfloat16)


def body(
    req_size, grp_size,
    residual, suffix_proj, prefix_cache, owner_req, lengths, norm_gain, up_weight, down_weight
):
    slot_count = residual.shape[2]
    feature_count = residual.shape[3]
    prefix_count = prefix_cache.shape[3]
    head_count = HEADS
    head_size = feature_count // head_count
    live = jnp.arange(slot_count, dtype=jnp.int32) < lengths[0, 0]
    needed = layer_bytes(grp_size, slot_count, feature_count, up_weight.shape[0])
    if req_size == 4 and grp_size == 8 and needed <= VMEM_LIMIT * 15 // 16:
        combined = layer_fused(
            grp_size, owner_req, norm_gain, residual[0, 0], suffix_proj[0, 0], prefix_cache[0, 0],
            up_weight, down_weight,
        )
        return jnp.where(live[:, None], combined, jnp.zeros_like(combined))[None, None]
    block = suffix_proj[0, 0].reshape(3, slot_count, head_count, head_size)
    query_pos = prefix_count + jnp.arange(slot_count, dtype=jnp.int32)
    prefix_pos = jnp.arange(prefix_count, dtype=jnp.int32)
    group_index = lax.axis_index("grp")
    owner_index = lax.dynamic_index_in_dim(owner_req, group_index, 0, keepdims=False)
    cached = from_owner(prefix_cache[0, 0], req_size, owner_index)
    cached = [half.reshape(prefix_count, head_count, head_size) for half in cached]
    first = attend(block[0], cached[0], cached[1], prefix_pos, query_pos, False)
    second = attend(block[0], block[1], block[2], query_pos, query_pos, True)
    context = merge_parts(first, second)
    states = (residual[0, 0].astype(jnp.float32) + context).astype(jnp.bfloat16)
    normed = layer_norm(states, norm_gain)
    combined = mlp_plain(normed, states, up_weight, down_weight)
    output = jnp.where(live[:, None], combined, jnp.zeros_like(combined))
    return output[None, None]


def solution(mesh):
    placed = (
        P("req", "grp", None, None),
        P("req", "grp", None, None, None),
        P("req", "grp", None, None, None),
        P(),
        P("req", "grp"),
        P(),
        P("grp", None),
        P("grp", None),
    )
    return jax.shard_map(
        functools.partial(body, mesh.shape["req"], mesh.shape["grp"]),
        mesh=mesh, in_specs=placed, out_specs=P("req", "grp", None, None), check_vma=False
    )
```

```python
import functools
import math

import jax
import jax.numpy as jnp
from jax import lax
from jax.experimental import pallas as pl
from jax.experimental.pallas import tpu as pltpu
from jax.sharding import PartitionSpec as P

HEADS = 32


NORM_EPS = 1e-05


def swap_halves(half, bits, req_size, owner_index):
    mine = lax.axis_index("req")
    for bit in bits:
        pairs = [(r, r ^ (1 << bit)) for r in range(req_size)]
        other = lax.ppermute(half, "req", pairs)
        same = ((mine >> bit) & 1) == ((owner_index >> bit) & 1)
        half = jnp.where(same, half, other)
    return half


def from_owner(block, req_size, owner_index):
    bits = list(range(req_size.bit_length() - 1))
    keys = swap_halves(block[0], bits, req_size, owner_index)
    values = swap_halves(block[1], bits[::-1], req_size, owner_index)
    return keys, values


def head_slopes(head_count):
    return jnp.exp2(-8.0 * jnp.arange(1, head_count + 1, dtype=jnp.float32) / head_count)


def attend(queries, key_rows, value_rows, key_pos, query_pos, causal):
    head_size = queries.shape[2]
    scores = jnp.einsum("qhe,khe->hqk", queries, key_rows, preferred_element_type=jnp.float32)
    scores = scores * (1.0 / math.sqrt(head_size))
    offsets = (key_pos[None, :] - query_pos[:, None]).astype(jnp.float32)
    scores = scores + head_slopes(queries.shape[1])[:, None, None] * offsets[None, :, :]
    if causal:
        scores = jnp.where((key_pos[None, :] <= query_pos[:, None])[None], scores, -jnp.inf)
    row_max = jnp.max(scores, axis=2)
    weights = jnp.exp(scores - row_max[:, :, None])
    row_total = jnp.sum(weights, axis=2)
    context = jnp.einsum(
        "hqk,khe->qhe", weights.astype(jnp.bfloat16), value_rows, preferred_element_type=jnp.float32
    )
    return (row_max, row_total, context)


def merge_parts(first, second):
    joint_max = jnp.maximum(first[0], second[0])
    first_scale = jnp.exp(first[0] - joint_max)
    second_scale = jnp.exp(second[0] - joint_max)
    numer = first[2] * first_scale.T[:, :, None] + second[2] * second_scale.T[:, :, None]
    denom = first[1] * first_scale + second[1] * second_scale
    merged = numer / denom.T[:, :, None]
    return merged.reshape(merged.shape[0], merged.shape[1] * merged.shape[2])


def layer_norm(state, norm_gain):
    values = state.astype(jnp.float32)
    center = values - jnp.mean(values, axis=-1, keepdims=True)
    spread = jnp.mean(center * center, axis=-1, keepdims=True)
    return (center * lax.rsqrt(spread + NORM_EPS) * norm_gain).astype(jnp.bfloat16)


MESH = pl.DeviceIdType.MESH
AG_PARTS = 4
RS_PARTS = 4
UP_TILE = 512
DOWN_TILE = 512


def layer_kernel(
    chips, owner_ref, slope_ref, gain_ref, residual_ref, proj_hbm, cache_hbm, up_hbm, down_hbm,
    out_ref,
    xg, upv, dnv, hid, part, sib, line, xn, values_two,
    wsem, ag_recv, ag_send, sib_send, sib_recv, rs_send, rs_recv, swap_send, swap_recv,
):
    rows = xg.shape[2]
    width = xg.shape[3]
    units = upv.shape[0]
    ag_cols = width // AG_PARTS
    rs_rows = rows // RS_PARTS
    me = lax.axis_index("grp")
    z = me // 2
    c = me % 2
    twin = z * 2 + 1 - c
    has_left = z > 0
    has_right = z < chips - 1

    up_copy = pltpu.make_async_copy(up_hbm, upv, wsem.at[0])
    down_copy = pltpu.make_async_copy(down_hbm, dnv, wsem.at[1])
    queries, keys, values = part.at[0, 0], part.at[0, 1], part.at[1, 0]
    keys_own, values_own = part.at[1, 1], part.at[2, 0]
    keys_one, values_one, keys_two = part.at[2, 1], part.at[3, 0], part.at[3, 1]
    loads = [
        pltpu.make_async_copy(cache_hbm.at[0], keys_own, wsem.at[2]),
        pltpu.make_async_copy(cache_hbm.at[1], values_own, wsem.at[3]),
        pltpu.make_async_copy(proj_hbm.at[0], queries, wsem.at[4]),
        pltpu.make_async_copy(proj_hbm.at[1], keys, wsem.at[5]),
        pltpu.make_async_copy(proj_hbm.at[2], values, wsem.at[6]),
    ]
    for load in loads:
        load.start()

    r = lax.axis_index("req")
    low_bit, high_bit = r % 2, r // 2
    peer_low = r + 1 - 2 * low_bit
    peer_high = r + 2 - 4 * high_bit
    owner = owner_ref[me]
    same_low = (owner % 2) == low_bit
    same_high = (owner // 2) == high_bit

    barrier = pltpu.get_barrier_semaphore()
    pl.semaphore_signal(barrier, inc=1, device_id={"grp": twin}, device_id_type=MESH)
    for peer in (peer_low, peer_high):
        pl.semaphore_signal(barrier, inc=1, device_id={"req": peer}, device_id_type=MESH)

    @pl.when(has_left)
    def _():
        pl.semaphore_signal(barrier, inc=1, device_id={"grp": me - 2}, device_id_type=MESH)

    @pl.when(has_right)
    def _():
        pl.semaphore_signal(barrier, inc=1, device_id={"grp": me + 2}, device_id_type=MESH)

    @pl.when(jnp.logical_and(has_left, has_right))
    def _():
        pl.semaphore_wait(barrier, 5)

    @pl.when(jnp.logical_not(jnp.logical_and(has_left, has_right)))
    def _():
        pl.semaphore_wait(barrier, 4)

    def swap_copy(kind, i):
        cols = pl.ds(i * ag_cols, ag_cols)
        src, dst, peer = (
            (keys_own, keys_one, peer_low),
            (values_own, values_one, peer_high),
            (keys_one, keys_two, peer_high),
            (values_one, values_two, peer_low),
        )[kind]
        return pltpu.make_async_remote_copy(
            src_ref=src.at[:, cols], dst_ref=dst.at[:, cols],
            send_sem=swap_send.at[kind, i], recv_sem=swap_recv.at[kind, i],
            device_id={"req": peer}, device_id_type=MESH,
        )

    def swap_start(i):
        swap_copy(0, i).start()
        swap_copy(1, i).start()

    def swap_relay(i):
        cols = pl.ds(i * ag_cols, ag_cols)
        swap_copy(0, i).wait_recv()
        keys_one[:, cols] = lax.select(same_low, keys_own[:, cols], keys_one[:, cols])
        swap_copy(2, i).start()
        swap_copy(1, i).wait_recv()
        values_one[:, cols] = lax.select(same_high, values_own[:, cols], values_one[:, cols])
        swap_copy(3, i).start()
        if i + 2 < AG_PARTS:
            swap_start(i + 2)

    loads[0].wait()
    loads[1].wait()
    swap_start(0)
    swap_start(1)
    for load in loads[2:]:
        load.wait()
    up_copy.start()
    down_copy.start()

    def ag_copy(zb, cc, s, way, target):
        piece = xg.at[zb, cc, :, pl.ds(s * ag_cols, ag_cols)]
        return pltpu.make_async_remote_copy(
            src_ref=piece, dst_ref=piece,
            send_sem=ag_send.at[way, zb, s], recv_sem=ag_recv.at[zb, cc, s],
            device_id={"grp": target}, device_id_type=MESH,
        )

    def sib_copy(zb):
        return pltpu.make_async_remote_copy(
            src_ref=part.at[zb, 1 - c], dst_ref=sib.at[zb],
            send_sem=sib_send.at[zb], recv_sem=sib_recv.at[zb],
            device_id={"grp": twin}, device_id_type=MESH,
        )

    def rs_copy(zb, slot, q, target):
        span = pl.ds(q * rs_rows, rs_rows)
        return pltpu.make_async_remote_copy(
            src_ref=part.at[zb, c, span], dst_ref=line.at[slot, span],
            send_sem=rs_send.at[zb, q], recv_sem=rs_recv.at[slot, q],
            device_id={"grp": target}, device_id_type=MESH,
        )

    def forward(t):
        for d in range(1, chips):
            s = t - d
            if not 0 <= s < AG_PARTS:
                continue

            @pl.when(z - d >= 0)
            def _():
                ag_copy(z - d, c, s, 0, twin).wait_recv()

                @pl.when(has_right)
                def _():
                    ag_copy(z - d, c, s, 0, me + 2).start()

                ag_copy(z - d, c, s, 2, twin).start()

            @pl.when(z + d < chips)
            def _():
                ag_copy(z + d, c, s, 1, twin).wait_recv()

                @pl.when(has_left)
                def _():
                    ag_copy(z + d, c, s, 1, me - 2).start()

                ag_copy(z + d, c, s, 2, twin).start()

    query_at = lax.broadcasted_iota(jnp.int32, (rows, rows), 0)
    key_at = lax.broadcasted_iota(jnp.int32, (rows, rows), 1)
    offset = (key_at - query_at).astype(jnp.float32)
    causal = key_at <= query_at
    head_size = width // HEADS
    scale = 1.0 / math.sqrt(head_size)
    nt = (((1,), (1,)), ((), ()))

    def attend_head(h, carry):
        cols = pl.ds(pl.multiple_of(h * head_size, head_size), head_size)
        slope = slope_ref[h]
        query = queries[:, cols]
        old_keys = lax.select(same_high, keys_one[:, cols], keys_two[:, cols])
        old_values = lax.select(same_low, values_one[:, cols], values_two[:, cols])
        old = lax.dot_general(query, old_keys, nt, preferred_element_type=jnp.float32)
        new = lax.dot_general(query, keys[:, cols], nt, preferred_element_type=jnp.float32)
        old = old * scale + slope * (offset - float(rows))
        new = jnp.where(causal, new * scale + slope * offset, -jnp.inf)
        top = jnp.maximum(
            jnp.max(old, axis=1, keepdims=True), jnp.max(new, axis=1, keepdims=True)
        )
        old = jnp.exp(old - top)
        new = jnp.exp(new - top)
        total = jnp.sum(old, axis=1, keepdims=True) + jnp.sum(new, axis=1, keepdims=True)
        context = jnp.dot(
            old.astype(jnp.bfloat16), old_values, preferred_element_type=jnp.float32
        ) + jnp.dot(
            new.astype(jnp.bfloat16), values[:, cols], preferred_element_type=jnp.float32
        )
        state = residual_ref[:, cols].astype(jnp.float32) + context / total
        xg[z, c, :, cols] = state.astype(jnp.bfloat16)
        return carry

    heads = HEADS // AG_PARTS
    swap_relay(0)
    for s in range(AG_PARTS):
        if s + 1 < AG_PARTS:
            swap_relay(s + 1)
        swap_copy(2, s).wait_recv()
        swap_copy(3, s).wait_recv()
        lax.fori_loop(s * heads, (s + 1) * heads, attend_head, 0, unroll=4)

        @pl.when(has_right)
        def _():
            ag_copy(z, c, s, 0, me + 2).start()

        @pl.when(has_left)
        def _():
            ag_copy(z, c, s, 1, me - 2).start()

        ag_copy(z, c, s, 2, twin).start()
        forward(s)

    for s in range(AG_PARTS):
        for kind in range(4):
            swap_copy(kind, s).wait_send()
    up_copy.wait()
    down_copy.wait()

    def compute(zb):
        for s in range(AG_PARTS):
            ag_copy(zb, 1 - c, s, 2, twin).wait_recv()

        def norm_step(t, carry):
            span = pl.ds(pl.multiple_of((t % (rows // 16)) * 16, 16), 16)
            dest = pl.ds(pl.multiple_of(t * 16, 16), 16)
            raw = xg[zb, t // (rows // 16), span, :].astype(jnp.float32)
            center = raw - jnp.mean(raw, axis=1, keepdims=True)
            spread = jnp.mean(center * center, axis=1, keepdims=True)
            scaled = center * lax.rsqrt(spread + NORM_EPS) * gain_ref[...]
            xn[dest, :] = scaled.astype(jnp.bfloat16)
            return carry

        lax.fori_loop(0, 2 * rows // 16, norm_step, 0)

        def up_step(j, carry):
            cols = pl.ds(pl.multiple_of(j * UP_TILE, UP_TILE), UP_TILE)
            pre = lax.dot_general(
                xn[...], upv[cols, :],
                (((1,), (1,)), ((), ())), preferred_element_type=jnp.float32,
            )
            act = 0.5 * pre * (1.0 + lax.erf(pre * math.sqrt(0.5)))
            hid[:, cols] = act.astype(jnp.bfloat16)
            return carry

        lax.fori_loop(0, units // UP_TILE, up_step, 0)

        def down_step(j, carry):
            cols = pl.ds(pl.multiple_of(j * DOWN_TILE, DOWN_TILE), DOWN_TILE)
            term = jnp.dot(hid[...], dnv[:, cols], preferred_element_type=jnp.float32)
            part[zb, :, :, cols] = term.astype(jnp.bfloat16).reshape(2, rows, DOWN_TILE)
            return carry

        lax.fori_loop(0, width // DOWN_TILE, down_step, 0)
        sib_copy(zb).start()

    def add_line(zb, q, with_line):
        span = pl.ds(q * rs_rows, rs_rows)
        total = part[zb, c, span].astype(jnp.float32) + sib[zb, span].astype(jnp.float32)
        if with_line:
            total = total + line[zb, span].astype(jnp.float32)
        part[zb, c, span] = total.astype(jnp.bfloat16)

    def step(d, carry):
        inward = jnp.where(z < chips // 2, 1, -1)
        is_end = jnp.logical_or(z == 0, z == chips - 1)

        def side_step(side, inner):
            place = 2 * (d - 1) + side
            for at, t in ((0, AG_PARTS), (1, AG_PARTS + 1), (3, AG_PARTS + 2)):
                @pl.when(place == at)
                def _():
                    forward(t)

            own = jnp.logical_and(side == 1, d == jnp.where(is_end, chips, chips - 1))
            zb = jnp.where(own, z, z + inward * d * (1 - 2 * side))

            @pl.when(jnp.logical_and(zb >= 0, zb < chips))
            def _():
                compute(zb)

            return inner

        lax.fori_loop(0, 2, side_step, 0)

        to_right = d
        to_left = chips - 1 - d
        goes_right = jnp.logical_and(z < to_right, d < chips)
        goes_left = jnp.logical_and(z > to_left, d < chips)

        @pl.when(goes_right)
        def _():
            sib_copy(to_right).wait_recv()

        @pl.when(goes_left)
        def _():
            sib_copy(to_left).wait_recv()

        for q in range(RS_PARTS):
            @pl.when(goes_right)
            def _():
                @pl.when(has_left)
                def _():
                    rs_copy(to_right, to_right, q, twin).wait_recv()
                    add_line(to_right, q, True)

                @pl.when(jnp.logical_not(has_left))
                def _():
                    add_line(to_right, q, False)

                rs_copy(to_right, to_right, q, me + 2).start()

            @pl.when(goes_left)
            def _():
                @pl.when(has_right)
                def _():
                    rs_copy(to_left, to_left, q, twin).wait_recv()
                    add_line(to_left, q, True)

                @pl.when(jnp.logical_not(has_right))
                def _():
                    add_line(to_left, q, False)

                @pl.when(z - 1 == to_left)
                def _():
                    rs_copy(to_left, chips, q, me - 2).start()

                @pl.when(z - 1 > to_left)
                def _():
                    rs_copy(to_left, to_left, q, me - 2).start()

        return carry

    lax.fori_loop(1, chips + 1, step, 0)

    sib_copy(z).wait_recv()
    for q in range(RS_PARTS):
        span = pl.ds(q * rs_rows, rs_rows)

        @pl.when(has_left)
        def _():
            rs_copy(z, z, q, twin).wait_recv()

        @pl.when(has_right)
        def _():
            rs_copy(z, chips, q, twin).wait_recv()

        def finish(slots):
            total = part[z, c, span].astype(jnp.float32) + sib[z, span].astype(jnp.float32)
            for slot in slots:
                total = total + line[slot, span].astype(jnp.float32)
            total = total + xg[z, c, span, :].astype(jnp.float32)
            out_ref[span] = total.astype(jnp.bfloat16)

        @pl.when(jnp.logical_and(has_left, has_right))
        def _():
            finish([z, chips])

        @pl.when(jnp.logical_not(has_left))
        def _():
            finish([chips])

        @pl.when(jnp.logical_not(has_right))
        def _():
            finish([z])

    def drain(zb, carry):
        for s in range(AG_PARTS):
            @pl.when(jnp.logical_and(has_right, zb <= z))
            def _():
                ag_copy(zb, c, s, 0, twin).wait_send()

            @pl.when(jnp.logical_and(has_left, zb >= z))
            def _():
                ag_copy(zb, c, s, 1, twin).wait_send()

            ag_copy(zb, c, s, 2, twin).wait_send()
        sib_copy(zb).wait_send()
        for q in range(RS_PARTS):
            @pl.when(zb != z)
            def _():
                rs_copy(zb, zb, q, twin).wait_send()
        return carry

    lax.fori_loop(0, chips, drain, 0)


def layer_bytes(grp_size, rows, width, units):
    chips = grp_size // 2
    blocks = 2 * chips + 2 * chips + chips + chips + 1 + 5
    return 2 * width * (blocks * rows + 2 * units) + 4 * rows * units


VMEM_LIMIT = 60 * 1024 * 1024


def layer_fused(
    grp_size, owner_req, norm_gain, residual, suffix_proj, prefix_cache, up_weight, down_weight
):
    chips = grp_size // 2
    rows, width = residual.shape
    units = up_weight.shape[0]
    bf16 = jnp.bfloat16
    dma = pltpu.SemaphoreType.DMA
    total_rows = rows * grp_size
    return pl.pallas_call(
        functools.partial(layer_kernel, chips),
        out_shape=jax.ShapeDtypeStruct((rows, width), bf16),
        in_specs=[
            pl.BlockSpec(memory_space=pltpu.SMEM),
            pl.BlockSpec(memory_space=pltpu.SMEM),
            pl.BlockSpec(memory_space=pltpu.VMEM),
            pl.BlockSpec(memory_space=pltpu.VMEM),
            pl.BlockSpec(memory_space=pl.ANY),
            pl.BlockSpec(memory_space=pl.ANY),
            pl.BlockSpec(memory_space=pl.ANY),
            pl.BlockSpec(memory_space=pl.ANY),
        ],
        out_specs=pl.BlockSpec(memory_space=pltpu.VMEM),
        scratch_shapes=[
            pltpu.VMEM((chips, 2, rows, width), bf16),
            pltpu.VMEM((units, width), bf16),
            pltpu.VMEM((units, width), bf16),
            pltpu.VMEM((2 * rows, units), bf16),
            pltpu.VMEM((chips, 2, rows, width), bf16),
            pltpu.VMEM((chips, rows, width), bf16),
            pltpu.VMEM((chips + 1, rows, width), bf16),
            pltpu.VMEM((2 * rows, width), bf16),
            pltpu.VMEM((rows, width), bf16),
            dma((7,)),
            dma((chips, 2, AG_PARTS)),
            dma((3, chips, AG_PARTS)),
            dma((chips,)),
            dma((chips,)),
            dma((chips, RS_PARTS)),
            dma((chips + 1, RS_PARTS)),
            dma((4, AG_PARTS)),
            dma((4, AG_PARTS)),
        ],
        compiler_params=pltpu.CompilerParams(
            collective_id=0, has_side_effects=True, vmem_limit_bytes=VMEM_LIMIT
        ),
        cost_estimate=pl.CostEstimate(
            flops=4 * total_rows * width * units,
            bytes_accessed=4 * units * width,
            transcendentals=total_rows * units,
        ),
    )(
        owner_req, head_slopes(HEADS), norm_gain[None, :], residual, suffix_proj, prefix_cache,
        up_weight, down_weight,
    )


def mlp_plain(normed, states, up_weight, down_weight):
    preactivation = lax.dot_general(
        lax.all_gather(normed, "grp", axis=0, tiled=True),
        up_weight,
        (((1,), (1,)), ((), ())),
        preferred_element_type=jnp.float32,
    )
    hidden = jax.nn.gelu(preactivation, approximate=False).astype(jnp.bfloat16)
    partial_term = jnp.dot(hidden, down_weight, preferred_element_type=jnp.float32).astype(
        jnp.bfloat16
    )
    mlp_sum = lax.psum_scatter(partial_term, "grp", scatter_dimension=0, tiled=True)
    return (states.astype(jnp.float32) + mlp_sum.astype(jnp.float32)).astype(jnp.bfloat16)


def body(
    req_size, grp_size,
    residual, suffix_proj, prefix_cache, owner_req, lengths, norm_gain, up_weight, down_weight
):
    slot_count = residual.shape[2]
    feature_count = residual.shape[3]
    prefix_count = prefix_cache.shape[3]
    head_count = HEADS
    head_size = feature_count // head_count
    live = jnp.arange(slot_count, dtype=jnp.int32) < lengths[0, 0]
    needed = layer_bytes(grp_size, slot_count, feature_count, up_weight.shape[0])
    if req_size == 4 and grp_size == 8 and needed <= VMEM_LIMIT * 15 // 16:
        combined = layer_fused(
            grp_size, owner_req, norm_gain, residual[0, 0], suffix_proj[0, 0], prefix_cache[0, 0],
            up_weight, down_weight,
        )
        return jnp.where(live[:, None], combined, jnp.zeros_like(combined))[None, None]
    block = suffix_proj[0, 0].reshape(3, slot_count, head_count, head_size)
    query_pos = prefix_count + jnp.arange(slot_count, dtype=jnp.int32)
    prefix_pos = jnp.arange(prefix_count, dtype=jnp.int32)
    group_index = lax.axis_index("grp")
    owner_index = lax.dynamic_index_in_dim(owner_req, group_index, 0, keepdims=False)
    cached = from_owner(prefix_cache[0, 0], req_size, owner_index)
    cached = [half.reshape(prefix_count, head_count, head_size) for half in cached]
    first = attend(block[0], cached[0], cached[1], prefix_pos, query_pos, False)
    second = attend(block[0], block[1], block[2], query_pos, query_pos, True)
    context = merge_parts(first, second)
    states = (residual[0, 0].astype(jnp.float32) + context).astype(jnp.bfloat16)
    normed = layer_norm(states, norm_gain)
    combined = mlp_plain(normed, states, up_weight, down_weight)
    output = jnp.where(live[:, None], combined, jnp.zeros_like(combined))
    return output[None, None]


def solution(mesh):
    placed = (
        P("req", "grp", None, None),
        P("req", "grp", None, None, None),
        P("req", "grp", None, None, None),
        P(),
        P("req", "grp"),
        P(),
        P("grp", None),
        P("grp", None),
    )
    return jax.shard_map(
        functools.partial(body, mesh.shape["req"], mesh.shape["grp"]),
        mesh=mesh, in_specs=placed, out_specs=P("req", "grp", None, None), check_vma=False
    )
```

```python
import functools
import math

import jax
import jax.numpy as jnp
from jax import lax
from jax.experimental import pallas as pl
from jax.experimental.pallas import tpu as pltpu
from jax.sharding import PartitionSpec as P

HEADS = 32


NORM_EPS = 1e-05


def swap_halves(half, bits, req_size, owner_index):
    mine = lax.axis_index("req")
    for bit in bits:
        pairs = [(r, r ^ (1 << bit)) for r in range(req_size)]
        other = lax.ppermute(half, "req", pairs)
        same = ((mine >> bit) & 1) == ((owner_index >> bit) & 1)
        half = jnp.where(same, half, other)
    return half


def from_owner(block, req_size, owner_index):
    bits = list(range(req_size.bit_length() - 1))
    keys = swap_halves(block[0], bits, req_size, owner_index)
    values = swap_halves(block[1], bits[::-1], req_size, owner_index)
    return keys, values


def head_slopes(head_count):
    return jnp.exp2(-8.0 * jnp.arange(1, head_count + 1, dtype=jnp.float32) / head_count)


def attend(queries, key_rows, value_rows, key_pos, query_pos, causal):
    head_size = queries.shape[2]
    scores = jnp.einsum("qhe,khe->hqk", queries, key_rows, preferred_element_type=jnp.float32)
    scores = scores * (1.0 / math.sqrt(head_size))
    offsets = (key_pos[None, :] - query_pos[:, None]).astype(jnp.float32)
    scores = scores + head_slopes(queries.shape[1])[:, None, None] * offsets[None, :, :]
    if causal:
        scores = jnp.where((key_pos[None, :] <= query_pos[:, None])[None], scores, -jnp.inf)
    row_max = jnp.max(scores, axis=2)
    weights = jnp.exp(scores - row_max[:, :, None])
    row_total = jnp.sum(weights, axis=2)
    context = jnp.einsum(
        "hqk,khe->qhe", weights.astype(jnp.bfloat16), value_rows, preferred_element_type=jnp.float32
    )
    return (row_max, row_total, context)


def merge_parts(first, second):
    joint_max = jnp.maximum(first[0], second[0])
    first_scale = jnp.exp(first[0] - joint_max)
    second_scale = jnp.exp(second[0] - joint_max)
    numer = first[2] * first_scale.T[:, :, None] + second[2] * second_scale.T[:, :, None]
    denom = first[1] * first_scale + second[1] * second_scale
    merged = numer / denom.T[:, :, None]
    return merged.reshape(merged.shape[0], merged.shape[1] * merged.shape[2])


def layer_norm(state, norm_gain):
    values = state.astype(jnp.float32)
    center = values - jnp.mean(values, axis=-1, keepdims=True)
    spread = jnp.mean(center * center, axis=-1, keepdims=True)
    return (center * lax.rsqrt(spread + NORM_EPS) * norm_gain).astype(jnp.bfloat16)


MESH = pl.DeviceIdType.MESH
AG_PARTS = 4
RS_PARTS = 4
UP_TILE = 512
DOWN_TILE = 512


def layer_kernel(
    chips, owner_ref, slope_ref, gain_ref, residual_ref, proj_hbm, cache_hbm, up_hbm, down_hbm,
    out_ref,
    xg, upv, dnv, hid, part, sib, line, xn, xt, values_two,
    wsem, ag_recv, ag_send, sib_send, sib_recv, rs_send, rs_recv, swap_send, swap_recv,
):
    rows = xg.shape[2]
    width = xg.shape[3]
    units = upv.shape[0]
    ag_cols = width // AG_PARTS
    rs_rows = rows // RS_PARTS
    me = lax.axis_index("grp")
    z = me // 2
    c = me % 2
    twin = z * 2 + 1 - c
    has_left = z > 0
    has_right = z < chips - 1

    up_copy = pltpu.make_async_copy(up_hbm, upv, wsem.at[0])
    down_copy = pltpu.make_async_copy(down_hbm, dnv, wsem.at[1])
    queries, keys, values = part.at[0, 0], part.at[0, 1], part.at[1, 0]
    keys_own, values_own = part.at[1, 1], part.at[2, 0]
    keys_one, values_one, keys_two = part.at[2, 1], part.at[3, 0], part.at[3, 1]
    loads = [
        pltpu.make_async_copy(cache_hbm.at[0], keys_own, wsem.at[2]),
        pltpu.make_async_copy(cache_hbm.at[1], values_own, wsem.at[3]),
        pltpu.make_async_copy(proj_hbm.at[0], queries, wsem.at[4]),
        pltpu.make_async_copy(proj_hbm.at[1], keys, wsem.at[5]),
        pltpu.make_async_copy(proj_hbm.at[2], values, wsem.at[6]),
    ]
    for load in loads:
        load.start()

    r = lax.axis_index("req")
    low_bit, high_bit = r % 2, r // 2
    peer_low = r + 1 - 2 * low_bit
    peer_high = r + 2 - 4 * high_bit
    owner = owner_ref[me]
    same_low = (owner % 2) == low_bit
    same_high = (owner // 2) == high_bit

    barrier = pltpu.get_barrier_semaphore()
    pl.semaphore_signal(barrier, inc=1, device_id={"grp": twin}, device_id_type=MESH)
    for peer in (peer_low, peer_high):
        pl.semaphore_signal(barrier, inc=1, device_id={"req": peer}, device_id_type=MESH)

    @pl.when(has_left)
    def _():
        pl.semaphore_signal(barrier, inc=1, device_id={"grp": me - 2}, device_id_type=MESH)

    @pl.when(has_right)
    def _():
        pl.semaphore_signal(barrier, inc=1, device_id={"grp": me + 2}, device_id_type=MESH)

    @pl.when(jnp.logical_and(has_left, has_right))
    def _():
        pl.semaphore_wait(barrier, 5)

    @pl.when(jnp.logical_not(jnp.logical_and(has_left, has_right)))
    def _():
        pl.semaphore_wait(barrier, 4)

    def swap_copy(kind, i):
        cols = pl.ds(i * ag_cols, ag_cols)
        src, dst, peer = (
            (keys_own, keys_one, peer_low),
            (values_own, values_one, peer_high),
            (keys_one, keys_two, peer_high),
            (values_one, values_two, peer_low),
        )[kind]
        return pltpu.make_async_remote_copy(
            src_ref=src.at[:, cols], dst_ref=dst.at[:, cols],
            send_sem=swap_send.at[kind, i], recv_sem=swap_recv.at[kind, i],
            device_id={"req": peer}, device_id_type=MESH,
        )

    def swap_start(i):
        swap_copy(0, i).start()
        swap_copy(1, i).start()

    def swap_relay(i):
        cols = pl.ds(i * ag_cols, ag_cols)
        swap_copy(0, i).wait_recv()
        keys_one[:, cols] = lax.select(same_low, keys_own[:, cols], keys_one[:, cols])
        swap_copy(2, i).start()
        swap_copy(1, i).wait_recv()
        values_one[:, cols] = lax.select(same_high, values_own[:, cols], values_one[:, cols])
        swap_copy(3, i).start()
        if i + 2 < AG_PARTS:
            swap_start(i + 2)

    loads[0].wait()
    loads[1].wait()
    swap_start(0)
    swap_start(1)
    for load in loads[2:]:
        load.wait()
    up_copy.start()
    down_copy.start()

    def ag_copy(zb, cc, s, way, target):
        piece = xg.at[zb, cc, :, pl.ds(s * ag_cols, ag_cols)]
        return pltpu.make_async_remote_copy(
            src_ref=piece, dst_ref=piece,
            send_sem=ag_send.at[way, zb, s], recv_sem=ag_recv.at[zb, cc, s],
            device_id={"grp": target}, device_id_type=MESH,
        )

    def sib_copy(zb):
        return pltpu.make_async_remote_copy(
            src_ref=part.at[zb, 1 - c], dst_ref=sib.at[zb],
            send_sem=sib_send.at[zb], recv_sem=sib_recv.at[zb],
            device_id={"grp": twin}, device_id_type=MESH,
        )

    def rs_copy(zb, slot, q, target):
        span = pl.ds(q * rs_rows, rs_rows)
        return pltpu.make_async_remote_copy(
            src_ref=part.at[zb, c, span], dst_ref=line.at[slot, span],
            send_sem=rs_send.at[zb, q], recv_sem=rs_recv.at[slot, q],
            device_id={"grp": target}, device_id_type=MESH,
        )

    def forward(t):
        for d in range(1, chips):
            s = t - d
            if not 0 <= s < AG_PARTS:
                continue

            @pl.when(z - d >= 0)
            def _():
                ag_copy(z - d, c, s, 0, twin).wait_recv()

                @pl.when(has_right)
                def _():
                    ag_copy(z - d, c, s, 0, me + 2).start()

                ag_copy(z - d, c, s, 2, twin).start()

            @pl.when(z + d < chips)
            def _():
                ag_copy(z + d, c, s, 1, twin).wait_recv()

                @pl.when(has_left)
                def _():
                    ag_copy(z + d, c, s, 1, me - 2).start()

                ag_copy(z + d, c, s, 2, twin).start()

    query_at = lax.broadcasted_iota(jnp.int32, (rows, rows), 0)
    key_at = lax.broadcasted_iota(jnp.int32, (rows, rows), 1)
    offset = (key_at - query_at).astype(jnp.float32)
    causal = key_at <= query_at
    head_size = width // HEADS
    scale = 1.0 / math.sqrt(head_size)
    nt = (((1,), (1,)), ((), ()))

    def attend_head(h, carry):
        cols = pl.ds(pl.multiple_of(h * head_size, head_size), head_size)
        slope = slope_ref[h]
        query = queries[:, cols]
        old_keys = lax.select(same_high, keys_one[:, cols], keys_two[:, cols])
        old_values = lax.select(same_low, values_one[:, cols], values_two[:, cols])
        old = lax.dot_general(query, old_keys, nt, preferred_element_type=jnp.float32)
        new = lax.dot_general(query, keys[:, cols], nt, preferred_element_type=jnp.float32)
        old = old * scale + slope * (offset - float(rows))
        new = jnp.where(causal, new * scale + slope * offset, -jnp.inf)
        top = jnp.maximum(
            jnp.max(old, axis=1, keepdims=True), jnp.max(new, axis=1, keepdims=True)
        )
        old = jnp.exp(old - top)
        new = jnp.exp(new - top)
        total = jnp.sum(old, axis=1, keepdims=True) + jnp.sum(new, axis=1, keepdims=True)
        context = jnp.dot(
            old.astype(jnp.bfloat16), old_values, preferred_element_type=jnp.float32
        ) + jnp.dot(
            new.astype(jnp.bfloat16), values[:, cols], preferred_element_type=jnp.float32
        )
        state = residual_ref[:, cols].astype(jnp.float32) + context / total
        xg[z, c, :, cols] = state.astype(jnp.bfloat16)
        return carry

    heads = HEADS // AG_PARTS
    swap_relay(0)
    for s in range(AG_PARTS):
        if s + 1 < AG_PARTS:
            swap_relay(s + 1)
        swap_copy(2, s).wait_recv()
        swap_copy(3, s).wait_recv()
        lax.fori_loop(s * heads, (s + 1) * heads, attend_head, 0, unroll=2)

        @pl.when(has_right)
        def _():
            ag_copy(z, c, s, 0, me + 2).start()

        @pl.when(has_left)
        def _():
            ag_copy(z, c, s, 1, me - 2).start()

        ag_copy(z, c, s, 2, twin).start()
        forward(s)

    for s in range(AG_PARTS):
        for kind in range(4):
            swap_copy(kind, s).wait_send()
    up_copy.wait()
    down_copy.wait()

    def compute(zb):
        for s in range(AG_PARTS):
            ag_copy(zb, 1 - c, s, 2, twin).wait_recv()

        def norm_step(t, carry):
            span = pl.ds(pl.multiple_of((t % (rows // 16)) * 16, 16), 16)
            dest = pl.ds(pl.multiple_of(t * 16, 16), 16)
            raw = xg[zb, t // (rows // 16), span, :].astype(jnp.float32)
            center = raw - jnp.mean(raw, axis=1, keepdims=True)
            spread = jnp.mean(center * center, axis=1, keepdims=True)
            scaled = center * lax.rsqrt(spread + NORM_EPS) * gain_ref[...]
            xn[dest, :] = scaled.astype(jnp.bfloat16)
            return carry

        lax.fori_loop(0, 2 * rows // 16, norm_step, 0)

        def turn_step(j, carry):
            cols = pl.ds(pl.multiple_of(j * UP_TILE, UP_TILE), UP_TILE)
            xt[cols, :] = xn[:, cols].T
            return carry

        lax.fori_loop(0, width // UP_TILE, turn_step, 0)

        def up_step(j, carry):
            cols = pl.ds(pl.multiple_of(j * UP_TILE, UP_TILE), UP_TILE)
            pre = jnp.dot(upv[cols, :], xt[...], preferred_element_type=jnp.float32)
            act = 0.5 * pre * (1.0 + lax.erf(pre * math.sqrt(0.5)))
            hid[:, cols] = act.astype(jnp.bfloat16).T
            return carry

        lax.fori_loop(0, units // UP_TILE, up_step, 0)

        def down_step(j, carry):
            cols = pl.ds(pl.multiple_of(j * DOWN_TILE, DOWN_TILE), DOWN_TILE)
            term = jnp.dot(hid[...], dnv[:, cols], preferred_element_type=jnp.float32)
            part[zb, :, :, cols] = term.astype(jnp.bfloat16).reshape(2, rows, DOWN_TILE)
            return carry

        lax.fori_loop(0, width // DOWN_TILE, down_step, 0)
        sib_copy(zb).start()

    def add_line(zb, q, with_line):
        span = pl.ds(q * rs_rows, rs_rows)
        total = part[zb, c, span].astype(jnp.float32) + sib[zb, span].astype(jnp.float32)
        if with_line:
            total = total + line[zb, span].astype(jnp.float32)
        part[zb, c, span] = total.astype(jnp.bfloat16)

    def step(d, carry):
        inward = jnp.where(z < chips // 2, 1, -1)
        is_end = jnp.logical_or(z == 0, z == chips - 1)

        def side_step(side, inner):
            place = 2 * (d - 1) + side
            for at, t in ((0, AG_PARTS), (1, AG_PARTS + 1), (3, AG_PARTS + 2)):
                @pl.when(place == at)
                def _():
                    forward(t)

            own = jnp.logical_and(side == 1, d == jnp.where(is_end, chips, chips - 1))
            zb = jnp.where(own, z, z + inward * d * (1 - 2 * side))

            @pl.when(jnp.logical_and(zb >= 0, zb < chips))
            def _():
                compute(zb)

            return inner

        lax.fori_loop(0, 2, side_step, 0)

        to_right = d
        to_left = chips - 1 - d
        goes_right = jnp.logical_and(z < to_right, d < chips)
        goes_left = jnp.logical_and(z > to_left, d < chips)

        @pl.when(goes_right)
        def _():
            sib_copy(to_right).wait_recv()

        @pl.when(goes_left)
        def _():
            sib_copy(to_left).wait_recv()

        for q in range(RS_PARTS):
            @pl.when(goes_right)
            def _():
                @pl.when(has_left)
                def _():
                    rs_copy(to_right, to_right, q, twin).wait_recv()
                    add_line(to_right, q, True)

                @pl.when(jnp.logical_not(has_left))
                def _():
                    add_line(to_right, q, False)

                rs_copy(to_right, to_right, q, me + 2).start()

            @pl.when(goes_left)
            def _():
                @pl.when(has_right)
                def _():
                    rs_copy(to_left, to_left, q, twin).wait_recv()
                    add_line(to_left, q, True)

                @pl.when(jnp.logical_not(has_right))
                def _():
                    add_line(to_left, q, False)

                @pl.when(z - 1 == to_left)
                def _():
                    rs_copy(to_left, chips, q, me - 2).start()

                @pl.when(z - 1 > to_left)
                def _():
                    rs_copy(to_left, to_left, q, me - 2).start()

        return carry

    lax.fori_loop(1, chips + 1, step, 0)

    sib_copy(z).wait_recv()
    for q in range(RS_PARTS):
        span = pl.ds(q * rs_rows, rs_rows)

        @pl.when(has_left)
        def _():
            rs_copy(z, z, q, twin).wait_recv()

        @pl.when(has_right)
        def _():
            rs_copy(z, chips, q, twin).wait_recv()

        def finish(slots):
            total = part[z, c, span].astype(jnp.float32) + sib[z, span].astype(jnp.float32)
            for slot in slots:
                total = total + line[slot, span].astype(jnp.float32)
            total = total + xg[z, c, span, :].astype(jnp.float32)
            out_ref[span] = total.astype(jnp.bfloat16)

        @pl.when(jnp.logical_and(has_left, has_right))
        def _():
            finish([z, chips])

        @pl.when(jnp.logical_not(has_left))
        def _():
            finish([chips])

        @pl.when(jnp.logical_not(has_right))
        def _():
            finish([z])

    def drain(zb, carry):
        for s in range(AG_PARTS):
            @pl.when(jnp.logical_and(has_right, zb <= z))
            def _():
                ag_copy(zb, c, s, 0, twin).wait_send()

            @pl.when(jnp.logical_and(has_left, zb >= z))
            def _():
                ag_copy(zb, c, s, 1, twin).wait_send()

            ag_copy(zb, c, s, 2, twin).wait_send()
        sib_copy(zb).wait_send()
        for q in range(RS_PARTS):
            @pl.when(zb != z)
            def _():
                rs_copy(zb, zb, q, twin).wait_send()
        return carry

    lax.fori_loop(0, chips, drain, 0)


def layer_bytes(grp_size, rows, width, units):
    chips = grp_size // 2
    blocks = 2 * chips + 2 * chips + chips + chips + 1 + 7
    return 2 * width * (blocks * rows + 2 * units) + 4 * rows * units


VMEM_LIMIT = 60 * 1024 * 1024


def layer_fused(
    grp_size, owner_req, norm_gain, residual, suffix_proj, prefix_cache, up_weight, down_weight
):
    chips = grp_size // 2
    rows, width = residual.shape
    units = up_weight.shape[0]
    bf16 = jnp.bfloat16
    dma = pltpu.SemaphoreType.DMA
    total_rows = rows * grp_size
    return pl.pallas_call(
        functools.partial(layer_kernel, chips),
        out_shape=jax.ShapeDtypeStruct((rows, width), bf16),
        in_specs=[
            pl.BlockSpec(memory_space=pltpu.SMEM),
            pl.BlockSpec(memory_space=pltpu.SMEM),
            pl.BlockSpec(memory_space=pltpu.VMEM),
            pl.BlockSpec(memory_space=pltpu.VMEM),
            pl.BlockSpec(memory_space=pl.ANY),
            pl.BlockSpec(memory_space=pl.ANY),
            pl.BlockSpec(memory_space=pl.ANY),
            pl.BlockSpec(memory_space=pl.ANY),
        ],
        out_specs=pl.BlockSpec(memory_space=pltpu.VMEM),
        scratch_shapes=[
            pltpu.VMEM((chips, 2, rows, width), bf16),
            pltpu.VMEM((units, width), bf16),
            pltpu.VMEM((units, width), bf16),
            pltpu.VMEM((2 * rows, units), bf16),
            pltpu.VMEM((chips, 2, rows, width), bf16),
            pltpu.VMEM((chips, rows, width), bf16),
            pltpu.VMEM((chips + 1, rows, width), bf16),
            pltpu.VMEM((2 * rows, width), bf16),
            pltpu.VMEM((width, 2 * rows), bf16),
            pltpu.VMEM((rows, width), bf16),
            dma((7,)),
            dma((chips, 2, AG_PARTS)),
            dma((3, chips, AG_PARTS)),
            dma((chips,)),
            dma((chips,)),
            dma((chips, RS_PARTS)),
            dma((chips + 1, RS_PARTS)),
            dma((4, AG_PARTS)),
            dma((4, AG_PARTS)),
        ],
        compiler_params=pltpu.CompilerParams(
            collective_id=0, has_side_effects=True, vmem_limit_bytes=VMEM_LIMIT
        ),
        cost_estimate=pl.CostEstimate(
            flops=4 * total_rows * width * units,
            bytes_accessed=4 * units * width,
            transcendentals=total_rows * units,
        ),
    )(
        owner_req, head_slopes(HEADS), norm_gain[None, :], residual, suffix_proj, prefix_cache,
        up_weight, down_weight,
    )


def mlp_plain(normed, states, up_weight, down_weight):
    preactivation = lax.dot_general(
        lax.all_gather(normed, "grp", axis=0, tiled=True),
        up_weight,
        (((1,), (1,)), ((), ())),
        preferred_element_type=jnp.float32,
    )
    hidden = jax.nn.gelu(preactivation, approximate=False).astype(jnp.bfloat16)
    partial_term = jnp.dot(hidden, down_weight, preferred_element_type=jnp.float32).astype(
        jnp.bfloat16
    )
    mlp_sum = lax.psum_scatter(partial_term, "grp", scatter_dimension=0, tiled=True)
    return (states.astype(jnp.float32) + mlp_sum.astype(jnp.float32)).astype(jnp.bfloat16)


def body(
    req_size, grp_size,
    residual, suffix_proj, prefix_cache, owner_req, lengths, norm_gain, up_weight, down_weight
):
    slot_count = residual.shape[2]
    feature_count = residual.shape[3]
    prefix_count = prefix_cache.shape[3]
    head_count = HEADS
    head_size = feature_count // head_count
    live = jnp.arange(slot_count, dtype=jnp.int32) < lengths[0, 0]
    needed = layer_bytes(grp_size, slot_count, feature_count, up_weight.shape[0])
    if req_size == 4 and grp_size == 8 and needed <= VMEM_LIMIT:
        combined = layer_fused(
            grp_size, owner_req, norm_gain, residual[0, 0], suffix_proj[0, 0], prefix_cache[0, 0],
            up_weight, down_weight,
        )
        return jnp.where(live[:, None], combined, jnp.zeros_like(combined))[None, None]
    block = suffix_proj[0, 0].reshape(3, slot_count, head_count, head_size)
    query_pos = prefix_count + jnp.arange(slot_count, dtype=jnp.int32)
    prefix_pos = jnp.arange(prefix_count, dtype=jnp.int32)
    group_index = lax.axis_index("grp")
    owner_index = lax.dynamic_index_in_dim(owner_req, group_index, 0, keepdims=False)
    cached = from_owner(prefix_cache[0, 0], req_size, owner_index)
    cached = [half.reshape(prefix_count, head_count, head_size) for half in cached]
    first = attend(block[0], cached[0], cached[1], prefix_pos, query_pos, False)
    second = attend(block[0], block[1], block[2], query_pos, query_pos, True)
    context = merge_parts(first, second)
    states = (residual[0, 0].astype(jnp.float32) + context).astype(jnp.bfloat16)
    normed = layer_norm(states, norm_gain)
    combined = mlp_plain(normed, states, up_weight, down_weight)
    output = jnp.where(live[:, None], combined, jnp.zeros_like(combined))
    return output[None, None]


def solution(mesh):
    placed = (
        P("req", "grp", None, None),
        P("req", "grp", None, None, None),
        P("req", "grp", None, None, None),
        P(),
        P("req", "grp"),
        P(),
        P("grp", None),
        P("grp", None),
    )
    return jax.shard_map(
        functools.partial(body, mesh.shape["req"], mesh.shape["grp"]),
        mesh=mesh, in_specs=placed, out_specs=P("req", "grp", None, None), check_vma=False
    )
```
